128 devices in a mesh: fsdp: 16 (over z, y), pre: 8 (over x, core).
Axes of the slice: x: 4, y: 4, z: 4, core: 2. Of those that a mesh axis runs over, the one named last changes fastest.
Arguments:
- inputs: bfloat16 [4096, 8192], P('fsdp', 'pre'), may hold values from -15 to 15
- grads_out: bfloat16 [4096, 8192], P('fsdp', 'pre'), may hold values from -0.234375 to 0.234375
- owner: int32 [16, 16], replicated, may hold values from 0 to 15, as said below
- offsets: int32 [16, 16], replicated, may hold values from 0 to 2, as said below
- prev_roots: float32 [384, 2, 512, 512], P(('fsdp', 'pre')), may hold values from -1 to 1, as said below
Outputs:
- update: bfloat16 [384, 512, 512], P(('fsdp', 'pre'))
- new_roots: float32 [384, 2, 512, 512], P(('fsdp', 'pre'))
The draws below stay inside these ranges and needn't reach their ends.
Inputs may be any that keep to these rules, and one draw needn't show every extreme that they name: Within each group of 2 block columns that one pre index holds, at most 3 blocks share an owner and some owner holds exactly 3; of the blocks in the rows of one fsdp index and one column group, at most 1 share an owner, and some reach 1. `offsets`: blocks of one column group with the same owner have distinct slots. `prev_roots`: each matrix is symmetric.
All inputs are finite; a program needn't handle non-finite values.
Results may differ from the reference program's by a relative error of at most 0.04.
Values may be sent and summed in bfloat16 or wider, within the bound.
No kernel may reach another device: no remote copies, remote signals or barrier semaphores. Data moves between devices by JAX's collectives and lax.ppermute only.
A program may use at most 192 MiB of HBM per device.

```python
import math
import jax
import jax.numpy as jnp
from jax import lax

BLOCK = 512
DIN = 8192
DOUT = 8192
TOK_DEV = 256
ITERS = 2
TOKENS = 4096
NBR = 16
NBC = 16
BRD = 1
BCD = 2
BLK_DEV = 2
PAIR = 1
CAP = 3
SLOTS_ALL = 384
N_FSDP = 16
N_PRE = 8


def assignment(seed_key):
    per_group = N_FSDP * BLK_DEV
    row_ids = jnp.arange(NBR, dtype=jnp.int32)[:, None]
    col_ids = jnp.arange(BCD, dtype=jnp.int32)[None, :]
    source = row_ids // BRD + 0 * col_ids
    local = row_ids % BRD * BCD + col_ids

    def one_group(group_key):
        first_key, second_key, third_key = jax.random.split(group_key, 3)
        source_keys = jax.random.split(first_key, N_FSDP)
        orders = jax.vmap(lambda k: jax.random.permutation(k, BLK_DEV).astype(jnp.int32))(source_keys)
        rank_in = orders[source, local]
        early = rank_in < PAIR
        even_source = source % 2 == 0
        base = jnp.where(even_source, jnp.where(early, source, source + 1), jnp.where(early, source - 1, (source + 1) % N_FSDP))
        shuffle = jax.random.permutation(second_key, N_FSDP).astype(jnp.int32)
        owners = shuffle[base]
        tie = jax.random.permutation(third_key, per_group).astype(jnp.int32).reshape(NBR, BCD)
        flat_owner = owners.reshape(-1)
        flat_tie = tie.reshape(-1)
        before = (flat_owner[None, :] == flat_owner[:, None]) & (flat_tie[None, :] < flat_tie[:, None])
        slot_of = jnp.sum(before.astype(jnp.int32), axis=1).reshape(NBR, BCD)
        return (owners.astype(jnp.int32), slot_of.astype(jnp.int32))
    group_keys = jax.random.split(seed_key, N_PRE)
    owners, slots_of = jax.vmap(one_group)(group_keys)
    owners = owners.transpose(1, 0, 2).reshape(NBR, NBC)
    slots_of = slots_of.transpose(1, 0, 2).reshape(NBR, NBC)
    return (owners.astype(jnp.int32), slots_of.astype(jnp.int32))


def draw_owner(seed_key, part_index):
    owners, slots_of = assignment(seed_key)
    return owners


def draw_offsets(seed_key, part_index):
    owners, slots_of = assignment(seed_key)
    return slots_of


def scaled_noise(noise_key, shape_of, width):
    scale_key, value_key = jax.random.split(noise_key)
    scales = jnp.exp(jax.random.uniform(scale_key, (width,), jnp.float32, 0.0, math.log(10.0)))
    values = jnp.clip(jax.random.normal(value_key, shape_of, jnp.float32), -6.0, 6.0)
    return values * scales[None, :] / 4.0


def draw_inputs(seed_key, part_index):
    seed_key = jax.random.fold_in(seed_key, 11)
    return scaled_noise(seed_key, (TOKENS, DIN), DIN).astype(jnp.bfloat16)


def draw_grads_out(seed_key, part_index):
    seed_key = jax.random.fold_in(seed_key, 23)
    values = scaled_noise(seed_key, (TOKENS, DOUT), DOUT) / math.sqrt(TOKENS)
    return values.astype(jnp.bfloat16)


def draw_prev_roots(seed_key, part_index):
    seed_key = jax.random.fold_in(seed_key, 37)
    shape_of = (SLOTS_ALL, 2, BLOCK, BLOCK)
    values = jnp.clip(jax.random.normal(seed_key, shape_of, jnp.float32), -6.0, 6.0)
    symmetric = (values + jnp.swapaxes(values, 2, 3)) * 0.5 * (0.2 / math.sqrt(BLOCK))
    return symmetric + 0.7 * jnp.eye(BLOCK, dtype=jnp.float32)


def setup_inputs(seed: int = 0) -> dict:
    arg_keys = jax.random.split(jax.random.key(seed), 6)
    return {
        "inputs": draw_inputs(jax.random.fold_in(arg_keys[5], 71), 0),
        "grads_out": draw_grads_out(jax.random.fold_in(arg_keys[5], 71), 0),
        "owner": draw_owner(jax.random.fold_in(arg_keys[5], 71), 0),
        "offsets": draw_offsets(jax.random.fold_in(arg_keys[5], 71), 0),
        "prev_roots": draw_prev_roots(jax.random.fold_in(arg_keys[5], 71), 0),
    }


def multiply(first_arg, second_arg):
    return jnp.dot(first_arg.astype(jnp.bfloat16), second_arg.astype(jnp.bfloat16), preferred_element_type=jnp.float32)


def newton(damped, previous):
    identity = jnp.eye(BLOCK, dtype=jnp.float32)
    square = multiply(previous, previous)
    fourth = multiply(square, square)
    product = multiply(fourth, damped)
    root_now = previous
    for iteration in range(ITERS):
        factor = (5.0 * identity - product) * 0.25
        factor_sq = multiply(factor, factor)
        factor_four = multiply(factor_sq, factor_sq)
        product = multiply(factor_four, product)
        root_now = multiply(root_now, factor)
    return root_now


def damp(statistic):
    scale = jnp.trace(statistic) / BLOCK + 1e-6
    return 0.1 * statistic / scale + jnp.eye(BLOCK, dtype=jnp.float32)


def solve_slot(operands):
    grad_block, previous = operands
    left_stat = jnp.dot(grad_block, grad_block.T, preferred_element_type=jnp.float32)
    right_stat = jnp.dot(grad_block.T, grad_block, preferred_element_type=jnp.float32)
    root_left = newton(damp(left_stat), previous[0])
    root_right = newton(damp(right_stat), previous[1])
    halfway = jnp.dot(root_left.astype(jnp.bfloat16), grad_block, preferred_element_type=jnp.float32).astype(jnp.bfloat16)
    result = jnp.dot(halfway, root_right.astype(jnp.bfloat16), preferred_element_type=jnp.float32).astype(jnp.bfloat16)
    return result, jnp.stack([root_left, root_right])


def reference(inputs, grads_out, owner, offsets, prev_roots):
    inputs_grouped = inputs.reshape(N_FSDP, TOK_DEV, DIN)
    outputs_grouped = grads_out.reshape(N_FSDP, TOK_DEV, DOUT)

    def accumulate(running, operands):
        partial_value = lax.dot_general(operands[0], operands[1], (((0,), (0,)), ((), ())), preferred_element_type=jnp.float32)
        rounded = lax.optimization_barrier(partial_value.astype(jnp.bfloat16))
        return running + rounded.astype(jnp.float32), None

    running, unused = lax.scan(accumulate, jnp.zeros((DIN, DOUT), jnp.float32), (inputs_grouped, outputs_grouped))
    gradient = running.astype(jnp.bfloat16)
    tiles = gradient.reshape(DIN // BLOCK, BLOCK, DOUT // BLOCK, BLOCK).transpose(0, 2, 1, 3).reshape(-1, BLOCK, BLOCK)
    columns = jnp.arange(DOUT // BLOCK, dtype=jnp.int32)
    slot_index = (owner * N_PRE + columns[None, :] // BCD) * CAP + offsets
    grad_slots = jnp.zeros((SLOTS_ALL, BLOCK, BLOCK), jnp.bfloat16).at[slot_index.reshape(-1).astype(jnp.int32)].set(tiles)
    update, new_roots = lax.map(solve_slot, (grad_slots, prev_roots))
    return update, new_roots
```

```python
import jax
import jax.numpy as jnp
from jax import lax
from jax.experimental import pallas as pl
from jax.experimental.pallas import tpu as pltpu
from jax.sharding import PartitionSpec as P

ITERS = 2
BF = jnp.bfloat16
F32 = jnp.float32
VMEM = 56 * 1024 * 1024


def dot(a, b):
    return jnp.dot(a, b, preferred_element_type=F32)


def params(**kw):
    return pltpu.CompilerParams(vmem_limit_bytes=VMEM, **kw)


def split_kernel(a_ref, o_ref):
    pieces, rows, tokens = o_ref.shape
    half = rows // 2
    flipped = a_ref[...].T
    for r in range(2):
        for f in range(pieces):
            start = r * pieces * half + f * half
            o_ref[f, r * half : (r + 1) * half, :] = flipped[start : start + half, :]


def split_features(a):
    tokens, feats = a.shape
    return pl.pallas_call(
        split_kernel,
        out_shape=jax.ShapeDtypeStruct((16, feats // 16, tokens), BF),
        compiler_params=params(),
    )(a)


def fourth_kernel(x_ref, xb_ref, f_ref):
    xb = x_ref[0].astype(BF)
    xb_ref[0] = xb
    sq = dot(xb, xb).astype(BF)
    f_ref[0] = dot(sq, sq).astype(BF)


def fourth_powers(roots):
    n, b, _ = roots.shape
    spec = pl.BlockSpec((1, b, b), lambda i: (i, 0, 0))
    return pl.pallas_call(
        fourth_kernel,
        grid=(n,),
        in_specs=[spec],
        out_specs=[spec, spec],
        out_shape=[jax.ShapeDtypeStruct((n, b, b), BF)] * 2,
        compiler_params=params(),
        cost_estimate=pl.CostEstimate(flops=4 * n * b**3, bytes_accessed=8 * n * b * b, transcendentals=0),
    )(roots)


def grad_kernel(me_ref, owner_ref, offs_ref, *refs):
    a_refs, (b_ref, o_ref, acc) = refs[:-3], refs[-3:]
    step = pl.program_id(0)
    chunk = a_refs[0].shape[0]
    rows = a_refs[0].shape[1]
    lhs = jnp.concatenate(
        [jnp.concatenate([a[j] for a in a_refs], axis=0) for j in range(chunk)], axis=1
    )
    part = dot(lhs, b_ref[...].reshape(lhs.shape[1], -1))

    @pl.when(step == 0)
    def _():
        acc[...] = part

    @pl.when(step > 0)
    def _():
        acc[...] += part

    @pl.when(step == pl.num_programs(0) - 1)
    def _():
        o_ref[...] = jnp.zeros_like(o_ref)
        me = me_ref[0]
        half = rows // 2
        block = o_ref.shape[2]
        for j in range(len(a_refs)):
            dx, dc = j // 2, j % 2
            p = 2 * lax.rem(me // 2 + dx, 4) + lax.rem(me % 2 + dc, 2)
            for r in range(2):
                for c in range(2):
                    key = owner_ref[2 * p + r, 2 * me + c] * 3 + offs_ref[2 * p + r, 2 * me + c]
                    o_ref[key] = acc[
                        j * rows + r * half : j * rows + (r + 1) * half, c * block : (c + 1) * block
                    ].astype(BF)


def gradient_pieces(me, owner, offsets, a_list, b):
    n, rows, tokens = a_list[0].shape
    cols = b.shape[1]
    chunk = 4
    smem = pl.BlockSpec(memory_space=pltpu.SMEM)
    return pl.pallas_call(
        grad_kernel,
        grid=(n // chunk,),
        in_specs=[smem] * 3
        + [pl.BlockSpec((chunk, rows, tokens), lambda i: (i, 0, 0))] * len(a_list)
        + [pl.BlockSpec((chunk * tokens, cols), lambda i: (i, 0))],
        out_specs=pl.BlockSpec((48, rows // 2, cols // 2), lambda i: (0, 0, 0)),
        out_shape=jax.ShapeDtypeStruct((48, rows // 2, cols // 2), BF),
        scratch_shapes=[pltpu.VMEM((len(a_list) * rows, cols), F32)],
        compiler_params=params(),
    )(me, owner, offsets, *a_list, b)


def newton_kernel(g_ref, xb_ref, f_ref, u_ref, n_ref):
    size = g_ref.shape[3]
    g = g_ref[...].reshape(size, size)
    gt = g.T
    g32 = g.astype(F32)
    scale = 0.1 / (jnp.sum(g32 * g32) / size + 1e-6)
    eye = (
        lax.broadcasted_iota(jnp.int32, (size, size), 0) == lax.broadcasted_iota(jnp.int32, (size, size), 1)
    ).astype(F32)
    roots = []
    for k in range(2):
        stat = dot(g, gt) if k == 0 else dot(gt, g)
        damped = (stat * scale + eye).astype(BF)
        m = dot(f_ref[0, k], damped)
        x = xb_ref[0, k]
        for it in range(ITERS):
            f = ((5.0 * eye - m) * 0.25).astype(BF)
            x32 = dot(x, f)
            x = x32.astype(BF)
            if it < ITERS - 1:
                f2 = dot(f, f).astype(BF)
                f4 = dot(f2, f2).astype(BF)
                m = dot(f4, m.astype(BF))
        n_ref[0, k] = x32
        roots.append(x)
    u_ref[0] = dot(dot(roots[0], g).astype(BF), roots[1]).astype(BF)


def newton(pieces, roots, fourth):
    n_src, slots, rows, b = pieces.shape
    pair = pl.BlockSpec((1, 2, b, b), lambda i: (i, 0, 0, 0))
    return pl.pallas_call(
        newton_kernel,
        grid=(slots,),
        in_specs=[pl.BlockSpec((n_src, 1, rows, b), lambda i: (0, i, 0, 0)), pair, pair],
        out_specs=[pl.BlockSpec((1, b, b), lambda i: (i, 0, 0)), pair],
        out_shape=[
            jax.ShapeDtypeStruct((slots, b, b), BF),
            jax.ShapeDtypeStruct((slots, 2, b, b), F32),
        ],
        compiler_params=params(),
    )(pieces, roots, fourth)


def gather_over_pre(s):
    up = [(2 * a + c, 2 * ((a + 1) % 4) + c) for a in range(4) for c in range(2)]
    down = [(b, a) for a, b in up]
    swap = [(2 * a + c, 2 * a + 1 - c) for a in range(4) for c in range(2)]
    h = s.shape[0] // 2
    from_below = lax.ppermute(s, "pre", up)
    from_above = lax.ppermute(s, "pre", down)
    far_a = lax.ppermute(from_below[:h], "pre", up)
    far_b = lax.ppermute(from_above[h:], "pre", down)
    far = jnp.concatenate([far_a, far_b], axis=0)
    out = []
    for one in (s, from_above, far, from_below):
        out += [one, lax.ppermute(one, "pre", swap)]
    return out


def body(inputs, grads_out, owner, offsets, prev_roots):
    slots, _, b, _ = prev_roots.shape
    tokens = inputs.shape[0]
    me = lax.axis_index("pre").astype(jnp.int32).reshape(1)
    b_all = lax.all_gather(grads_out, "fsdp", axis=0, tiled=True)
    mine = split_features(inputs)
    mine = lax.all_to_all(mine, "fsdp", 0, 0, tiled=True)
    a_list = gather_over_pre(mine)
    xb, fourth = fourth_powers(prev_roots.reshape(slots * 2, b, b))
    pieces = gradient_pieces(me, owner, offsets, a_list, b_all)
    pieces = lax.all_to_all(pieces, "fsdp", 0, 0, tiled=True)
    update, roots = newton(
        pieces.reshape(16, slots, -1, b), xb.reshape(slots, 2, b, b), fourth.reshape(slots, 2, b, b)
    )
    return update, roots


def solution(mesh):
    in_specs = (P("fsdp", "pre"), P("fsdp", "pre"), P(), P(), P(("fsdp", "pre"), None, None, None))
    out_specs = (P(("fsdp", "pre"), None, None), P(("fsdp", "pre"), None, None, None))
    return jax.shard_map(body, mesh=mesh, in_specs=in_specs, out_specs=out_specs, check_vma=False)
```

```python
import jax
import jax.numpy as jnp
from jax import lax
from jax.experimental import pallas as pl
from jax.experimental.pallas import tpu as pltpu
from jax.sharding import PartitionSpec as P

ITERS = 2
BF = jnp.bfloat16
F32 = jnp.float32
VMEM = 20 * 1024 * 1024
SHORT = pl.CostEstimate(flops=1, bytes_accessed=1, transcendentals=0)


def dot(a, b):
    return jnp.dot(a, b, preferred_element_type=F32)


def params(**kw):
    return pltpu.CompilerParams(vmem_limit_bytes=VMEM, **kw)


def split_kernel(core_ref, a_ref, r_ref, o_ref):
    pieces, rows, tokens = o_ref.shape
    part = rows // 4
    start = pl.multiple_of(core_ref[0] * tokens, tokens)
    for o in range(2):
        flipped = (a_ref[pl.ds(start, tokens), :] if o == 0 else r_ref[0]).T
        for r in range(2):
            for f in range(pieces):
                at, to = (r * pieces + f) * part, (2 * o + r) * part
                o_ref[f, to : to + part, :] = flipped[at : at + part, :]


def split_features(core, a, recv):
    tokens, feats = a.shape
    whole = lambda s: pl.BlockSpec(s, lambda i: (0,) * len(s))
    return pl.pallas_call(
        split_kernel,
        grid=(1,),
        in_specs=[pl.BlockSpec(memory_space=pltpu.SMEM), whole(a.shape), whole((1,) + recv.shape[1:])],
        out_specs=whole((16, feats // 8, tokens // 2)),
        out_shape=jax.ShapeDtypeStruct((16, feats // 8, tokens // 2), BF),
        compiler_params=params(),
        cost_estimate=SHORT,
    )(core, a, recv)


def fourth_kernel(x_ref, xb_ref, f_ref):
    xb = x_ref[0].astype(BF)
    xb_ref[0] = xb
    sq = dot(xb, xb).astype(BF)
    f_ref[0] = dot(sq, sq).astype(BF)


def fourth_powers(roots):
    n, b, _ = roots.shape
    spec = pl.BlockSpec((1, b, b), lambda i: (i, 0, 0))
    return pl.pallas_call(
        fourth_kernel,
        grid=(n,),
        in_specs=[spec],
        out_specs=[spec, spec],
        out_shape=[jax.ShapeDtypeStruct((n, b, b), BF)] * 2,
        compiler_params=params(),
        cost_estimate=SHORT,
    )(roots)


def join_kernel(*refs):
    for i, v in enumerate(refs[:-1]):
        refs[-1][i] = v[0]


def join(parts):
    n, rows, cols = parts[0].shape
    return pl.pallas_call(
        join_kernel,
        grid=(n,),
        in_specs=[pl.BlockSpec((1, rows, cols), lambda i: (i, 0, 0))] * len(parts),
        out_specs=pl.BlockSpec((len(parts), rows, cols), lambda i: (i, 0, 0)),
        out_shape=jax.ShapeDtypeStruct((n * len(parts), rows, cols), BF),
        compiler_params=params(),
        cost_estimate=SHORT,
    )(*parts)


def token_pieces(place_ref, j):
    z, y, core = place_ref[0], place_ref[1], place_ref[3]
    out = []
    for i in range(4):
        dz = jnp.where(core == 0, j, i)
        dy = jnp.where(core == 0, i, j)
        out.append(lax.rem(z + dz, 4) * 4 + lax.rem(y + dy, 4))
    return out


def left_operand(place_ref, a_refs, j):
    at = token_pieces(place_ref, j)
    rows = [jnp.concatenate([a[f] for f in at], axis=1) for a in a_refs]
    return jnp.concatenate(rows, axis=0)


def product(lhs, b):
    return dot(lhs, b.reshape(lhs.shape[1], b.shape[-1]))


def first_kernel(place_ref, *refs):
    a_refs, b_refs, o_ref, lhs = refs[:4], refs[4:7], refs[7], refs[-1]

    @pl.when(pl.program_id(0) == 0)
    def _():
        for n, j in enumerate((0, 1, 3)):
            lhs[n] = left_operand(place_ref, a_refs, j)
        if len(refs) == 10:
            refs[8][...] = left_operand(place_ref, a_refs, 2)

    o_ref[...] = sum(product(lhs[n], b_refs[n][...]) for n in range(3)).astype(o_ref.dtype)


def first_chunks(place, a_list, chunks, other):
    n, rows, tokens = a_list[0].shape
    cols = chunks[0].shape[-1]
    width = cols // 4
    full = (4 * rows, 4 * tokens)
    out_specs = [pl.BlockSpec((4 * rows, width), lambda i: (0, i))]
    out_shape = [jax.ShapeDtypeStruct((4 * rows, cols), BF if other else F32)]
    if other:
        out_specs.append(pl.BlockSpec(full, lambda i: (0, 0)))
        out_shape.append(jax.ShapeDtypeStruct(full, BF))
    return pl.pallas_call(
        first_kernel,
        grid=(cols // width,),
        in_specs=[pl.BlockSpec(memory_space=pltpu.SMEM)]
        + [pl.BlockSpec((n, rows, tokens), lambda i: (0, 0, 0))] * 4
        + [pl.BlockSpec((4, tokens, width), lambda i: (int(other), 0, i))] * 3,
        out_specs=out_specs,
        out_shape=out_shape,
        scratch_shapes=[pltpu.VMEM((3,) + full, BF)],
        compiler_params=params(),
        cost_estimate=SHORT,
    )(place, *a_list, *chunks)


def last_kernel(place_ref, owner_ref, offs_ref, lhs_ref, cross_ref, own_ref, far_ref, acc_ref, share_ref, o_ref):
    x, core = place_ref[2], place_ref[3]
    part, block = o_ref.shape[1:]
    o_ref[...] = jnp.zeros_like(o_ref)
    for c in range(2):
        at_cols = slice(c * block, (c + 1) * block)
        total = acc_ref[:, at_cols] + product(lhs_ref[...], own_ref[:, :, at_cols])
        cross = share_ref[:, at_cols].astype(F32) + product(cross_ref[...], far_ref[:, :, at_cols])
        col = 2 * (2 * x + core) + c
        for dx in range(4):
            for o in range(2):
                p = 2 * lax.rem(x + dx, 4) + lax.rem(core + o, 2)
                for r in range(2):
                    at = ((dx * 2 + o) * 2 + r) * part
                    to = ((dx * 2 + 1 - o) * 2 + r) * part
                    row = 2 * p + r
                    key = owner_ref[row, col] * 3 + offs_ref[row, col]
                    o_ref[key] = (total[at : at + part] + cross[to : to + part]).astype(BF)


def last_chunk(place, owner, offsets, lhs, cross_lhs, own, far, acc, share):
    rows, cols = acc.shape
    operands = (lhs, cross_lhs, own, far, acc, share)
    return pl.pallas_call(
        last_kernel,
        grid=(1,),
        in_specs=[pl.BlockSpec(memory_space=pltpu.SMEM)] * 3
        + [pl.BlockSpec(v.shape, lambda i, n=v.ndim: (0,) * n) for v in operands],
        out_specs=pl.BlockSpec((48, rows // 16, cols // 2), lambda i: (0, 0, 0)),
        out_shape=jax.ShapeDtypeStruct((48, rows // 16, cols // 2), BF),
        compiler_params=params(),
        cost_estimate=SHORT,
    )(place, owner, offsets, *operands)


def newton_kernel(g_ref, xb_ref, f_ref, u_ref, n_ref):
    size = g_ref.shape[3]
    g = g_ref[...].reshape(size, size)
    gt = g.T
    g32 = g.astype(F32)
    scale = 0.1 / (jnp.sum(g32 * g32) / size + 1e-6)
    eye = (
        lax.broadcasted_iota(jnp.int32, (size, size), 0) == lax.broadcasted_iota(jnp.int32, (size, size), 1)
    ).astype(F32)
    roots = []
    for k in range(2):
        stat = dot(g, gt) if k == 0 else dot(gt, g)
        damped = (stat * scale + eye).astype(BF)
        m = dot(f_ref[0, k], damped)
        x = xb_ref[0, k]
        for it in range(ITERS):
            f = ((5.0 * eye - m) * 0.25).astype(BF)
            x32 = dot(x, f)
            x = x32.astype(BF)
            if it < ITERS - 1:
                f2 = dot(f, f).astype(BF)
                f4 = dot(f2, f2).astype(BF)
                m = dot(f4, m.astype(BF))
        n_ref[0, k] = x32
        roots.append(x)
    u_ref[0] = dot(dot(roots[0], g).astype(BF), roots[1]).astype(BF)


def newton(pieces, roots, fourth):
    n_src, slots, rows, b = pieces.shape
    pair = pl.BlockSpec((1, 2, b, b), lambda i: (i, 0, 0, 0))
    return pl.pallas_call(
        newton_kernel,
        grid=(slots,),
        in_specs=[pl.BlockSpec((n_src, 1, rows, b), lambda i: (0, i, 0, 0)), pair, pair],
        out_specs=[pl.BlockSpec((1, b, b), lambda i: (i, 0, 0)), pair],
        out_shape=[
            jax.ShapeDtypeStruct((slots, b, b), BF),
            jax.ShapeDtypeStruct((slots, 2, b, b), F32),
        ],
        compiler_params=params(),
        cost_estimate=SHORT,
    )(pieces, roots, fourth)


def device(z, y, x, core):
    return ((z % 4) * 4 + y % 4) * 8 + (x % 4) * 2 + core


def chips():
    return [(z, y, x) for z in range(4) for y in range(4) for x in range(4)]


def swap_cores(v):
    return lax.ppermute(
        v, ("fsdp", "pre"), [(device(*p, c), device(*p, 1 - c)) for p in chips() for c in range(2)]
    )


def from_x(v, d):
    return lax.ppermute(
        v, ("fsdp", "pre"), [(device(z, y, x + d, c), device(z, y, x, c)) for z, y, x in chips() for c in range(2)]
    )


def from_ring(v, phase, d):
    pairs = []
    for z, y, x in chips():
        for c in range(2):
            dz, dy = (0, d) if phase == c else (d, 0)
            pairs.append((device(z + dz, y + dy, x, c), device(z, y, x, c)))
    return lax.ppermute(v, ("fsdp", "pre"), pairs)


def from_ring_across(v, d):
    pairs = []
    for z, y, x in chips():
        for c in range(2):
            dz, dy = (0, d) if c == 0 else (d, 0)
            pairs.append((device(z + dz, y + dy, x, 1 - c), device(z, y, x, c)))
    return lax.ppermute(v, ("fsdp", "pre"), pairs)


def body(inputs, grads_out, owner, offsets, prev_roots):
    slots, _, b, _ = prev_roots.shape
    tokens, cols = grads_out.shape
    half = tokens // 2
    f = lax.axis_index("fsdp").astype(jnp.int32)
    p = lax.axis_index("pre").astype(jnp.int32)
    core = p % 2
    place = jnp.stack([f // 4, f % 4, p // 2, core])
    rows_of = lambda v, c: lax.dynamic_slice_in_dim(v, c * half, half, 0)

    sent = jnp.stack([rows_of(inputs, 1 - core), rows_of(grads_out, 1 - core)])
    recv = swap_cores(sent)
    shard = jnp.stack([rows_of(grads_out, core), recv[1]])

    near = [shard, from_ring(shard, 0, 1), from_ring(shard, 0, 2), from_ring(shard, 0, 3)]
    both = join(near)

    mine = split_features(core.reshape(1), inputs, recv)
    mine = lax.all_to_all(mine, "fsdp", 0, 0, tiled=True)
    both, mine = lax.optimization_barrier((both, mine))
    up = from_ring(both, 1, 1)
    down = from_ring(both, 1, 3)
    a_list = [mine, from_x(mine, 1), from_x(mine, 2), from_x(mine, 3)]
    own_2 = from_ring(up[:4], 1, 1)
    far_2 = from_ring_across(down[4:], 3)

    xb, fourth = fourth_powers(prev_roots.reshape(slots * 2, b, b))
    share, lhs = first_chunks(place, a_list, [both, up, down], True)
    (acc,) = first_chunks(place, a_list, [both, up, down], False)
    pieces = last_chunk(
        place, owner, offsets, lhs, swap_cores(lhs), own_2, far_2, acc, swap_cores(share)
    )
    pieces = lax.all_to_all(pieces, "fsdp", 0, 0, tiled=True)
    update, roots = newton(
        pieces.reshape(16, slots, -1, b), xb.reshape(slots, 2, b, b), fourth.reshape(slots, 2, b, b)
    )
    return update, roots


def solution(mesh):
    in_specs = (P("fsdp", "pre"), P("fsdp", "pre"), P(), P(), P(("fsdp", "pre"), None, None, None))
    out_specs = (P(("fsdp", "pre"), None, None), P(("fsdp", "pre"), None, None, None))
    return jax.shard_map(body, mesh=mesh, in_specs=in_specs, out_specs=out_specs, check_vma=False)
```

```python
import jax
import jax.numpy as jnp
from jax import lax
from jax.experimental import pallas as pl
from jax.experimental.pallas import tpu as pltpu
from jax.sharding import PartitionSpec as P

ITERS = 2
BF = jnp.bfloat16
F32 = jnp.float32
VMEM = 12 * 1024 * 1024
MIDDLE_VMEM = 12 * 1024 * 1024
LARGE_VMEM = 20 * 1024 * 1024
SHORT = pl.CostEstimate(flops=1, bytes_accessed=1, transcendentals=0)


def dot(a, b):
    return jnp.dot(a, b, preferred_element_type=F32)


def params(**kw):
    return pltpu.CompilerParams(vmem_limit_bytes=VMEM, **kw)


def split_kernel(core_ref, a_ref, r_ref, o_ref):
    pieces, rows, tokens = o_ref.shape
    part = rows // 4
    start = pl.multiple_of(core_ref[0] * tokens, tokens)
    for o in range(2):
        flipped = (a_ref[pl.ds(start, tokens), :] if o == 0 else r_ref[0]).T
        for r in range(2):
            for f in range(pieces):
                at, to = (r * pieces + f) * part, (2 * o + r) * part
                o_ref[f, to : to + part, :] = flipped[at : at + part, :]


def split_features(core, a, recv):
    tokens, feats = a.shape
    whole = lambda s: pl.BlockSpec(s, lambda i: (0,) * len(s))
    return pl.pallas_call(
        split_kernel,
        grid=(1,),
        in_specs=[pl.BlockSpec(memory_space=pltpu.SMEM), whole(a.shape), whole((1,) + recv.shape[1:])],
        out_specs=whole((16, feats // 8, tokens // 2)),
        out_shape=jax.ShapeDtypeStruct((16, feats // 8, tokens // 2), BF),
        compiler_params=params(),
        cost_estimate=SHORT,
    )(core, a, recv)


def fourth_kernel(x_ref, xb_ref, f_ref):
    xb = x_ref[0].astype(BF)
    xb_ref[0] = xb
    sq = dot(xb, xb).astype(BF)
    f_ref[0] = dot(sq, sq).astype(BF)


def fourth_powers(roots):
    n, b, _ = roots.shape
    spec = pl.BlockSpec((1, b, b), lambda i: (i, 0, 0))
    return pl.pallas_call(
        fourth_kernel,
        grid=(n,),
        in_specs=[spec],
        out_specs=[spec, spec],
        out_shape=[pltpu.HBM((n, b, b), BF)] * 2,
        compiler_params=pltpu.CompilerParams(vmem_limit_bytes=MIDDLE_VMEM),
        cost_estimate=SHORT,
    )(roots)


def join_kernel(*refs):
    parts, o_ref = refs[:-1], refs[-1]
    for o in range(2):
        for i, v in enumerate(parts):
            o_ref[o * len(parts) + i] = v[o]


def join(parts):
    n, rows, cols = parts[0].shape
    vmem = pl.BlockSpec(memory_space=pltpu.VMEM)
    return pl.pallas_call(
        join_kernel,
        in_specs=[vmem] * len(parts),
        out_specs=vmem,
        out_shape=jax.ShapeDtypeStruct((n * len(parts), rows, cols), BF),
        compiler_params=params(),
        cost_estimate=SHORT,
    )(*parts)


def token_pieces(place_ref, j):
    z, y, core = place_ref[0], place_ref[1], place_ref[3]
    out = []
    for i in range(4):
        dz = jnp.where(core == 0, j, i)
        dy = jnp.where(core == 0, i, j)
        out.append(lax.rem(z + dz, 4) * 4 + lax.rem(y + dy, 4))
    return out


def left_operand(place_ref, a_refs, j):
    at = token_pieces(place_ref, j)
    rows = [jnp.concatenate([a[f] for f in at], axis=1) for a in a_refs]
    return jnp.concatenate(rows, axis=0)


def product(lhs, *b):
    return dot(lhs, jnp.concatenate([v.reshape(-1, v.shape[-1]) for v in b], axis=0))


def first_kernel(place_ref, *refs):
    a_refs, b_refs, shares, (acc_ref, last_ref) = refs[:4], refs[4:7], refs[7:9], refs[9:]
    lhs = jnp.concatenate([left_operand(place_ref, a_refs, j) for j in (0, 1, 3)], axis=1)
    block = shares[0].shape[1]
    for o in (1, 0):
        for c in range(2):
            at = slice(c * block, (c + 1) * block)
            total = product(lhs, *[v[4 * o : 4 * o + 4, :, at] for v in b_refs])
            if o:
                shares[c][...] = total.astype(BF)
            else:
                acc_ref[:, at] = total
    last_ref[...] = left_operand(place_ref, a_refs, 2)


def first_chunks(place, a_list, chunks):
    n, rows, tokens = a_list[0].shape
    cols = chunks[0].shape[-1]
    full = (4 * rows, 4 * tokens)
    vmem = pl.BlockSpec(memory_space=pltpu.VMEM)
    return pl.pallas_call(
        first_kernel,
        in_specs=[pl.BlockSpec(memory_space=pltpu.SMEM)] + [vmem] * 7,
        out_specs=[vmem] * 4,
        out_shape=[jax.ShapeDtypeStruct(full, BF)] * 2
        + [jax.ShapeDtypeStruct((4 * rows, cols), F32), jax.ShapeDtypeStruct(full, BF)],
        compiler_params=params(),
        cost_estimate=pl.CostEstimate(flops=3 * 2**30, bytes_accessed=12 * 2**20, transcendentals=0),
    )(place, *a_list, *chunks)


def last_kernel(place_ref, owner_ref, offs_ref, lhs_ref, cross_ref, own_ref, far_ref, acc_ref, share_0, share_1, o_ref):
    x, core = place_ref[2], place_ref[3]
    part, block = o_ref.shape[1:]
    o_ref[...] = jnp.zeros_like(o_ref)
    for c in range(2):
        at_cols = slice(c * block, (c + 1) * block)
        total = acc_ref[:, at_cols] + product(lhs_ref[...], own_ref[:, :, at_cols])
        cross = (share_0, share_1)[c][...].astype(F32) + product(cross_ref[...], far_ref[:, :, at_cols])
        col = 2 * (2 * x + core) + c
        for dx in range(4):
            for o in range(2):
                p = 2 * lax.rem(x + dx, 4) + lax.rem(core + o, 2)
                for r in range(2):
                    at = ((dx * 2 + o) * 2 + r) * part
                    to = ((dx * 2 + 1 - o) * 2 + r) * part
                    row = 2 * p + r
                    key = owner_ref[row, col] * 3 + offs_ref[row, col]
                    o_ref[key] = (total[at : at + part] + cross[to : to + part]).astype(BF)


def last_chunk(place, owner, offsets, *operands):
    rows, cols = operands[4].shape
    return pl.pallas_call(
        last_kernel,
        in_specs=[pl.BlockSpec(memory_space=pltpu.SMEM)] * 3
        + [pl.BlockSpec(memory_space=pltpu.VMEM)] * len(operands),
        out_specs=pl.BlockSpec(memory_space=pltpu.VMEM),
        out_shape=jax.ShapeDtypeStruct((48, rows // 16, cols // 2), BF),
        compiler_params=params(),
        cost_estimate=SHORT,
    )(place, owner, offsets, *operands)


def newton_kernel(g_ref, xb_ref, f_ref, u_ref, n_ref):
    size = g_ref.shape[3]
    g = g_ref[...].reshape(size, size)
    gt = g.T
    g32 = g.astype(F32)
    scale = 0.1 / (jnp.sum(g32 * g32) / size + 1e-6)
    rows, cols = (lax.broadcasted_iota(jnp.int32, (size, size), d) for d in range(2))
    diagonal = rows == cols
    stats = [dot(g, gt), dot(gt, g)]
    damped = [(v * scale + jnp.where(diagonal, 1.0, 0.0)).astype(BF) for v in stats]
    ms = [dot(f_ref[0, k], damped[k]) for k in range(2)]
    xs = [xb_ref[0, k] for k in range(2)]
    for it in range(ITERS):
        fs = [(jnp.where(diagonal, 5.0 - m, -m) * 0.25).astype(BF) for m in ms]
        if it < ITERS - 1:
            twos = [dot(f, f).astype(BF) for f in fs]
            xs = [dot(x, f).astype(BF) for x, f in zip(xs, fs)]
            fours = [dot(v, v).astype(BF) for v in twos]
            ms = [dot(v, m.astype(BF)) for v, m in zip(fours, ms)]
        else:
            xs = [dot(x, f) for x, f in zip(xs, fs)]
    for k in range(2):
        n_ref[0, k] = xs[k]
    left, right = (x.astype(BF) for x in xs)
    u_ref[0] = dot(dot(left, g).astype(BF), right).astype(BF)


def newton(pieces, roots, fourth):
    n_src, slots, rows, b = pieces.shape
    pair = pl.BlockSpec((1, 2, b, b), lambda i: (i, 0, 0, 0))
    return pl.pallas_call(
        newton_kernel,
        grid=(slots,),
        in_specs=[pl.BlockSpec((n_src, 1, rows, b), lambda i: (0, i, 0, 0)), pair, pair],
        out_specs=[pl.BlockSpec((1, b, b), lambda i: (i, 0, 0)), pair],
        out_shape=[
            jax.ShapeDtypeStruct((slots, b, b), BF),
            jax.ShapeDtypeStruct((slots, 2, b, b), F32),
        ],
        compiler_params=pltpu.CompilerParams(vmem_limit_bytes=LARGE_VMEM),
        cost_estimate=SHORT,
    )(pieces, roots, fourth)


def device(z, y, x, core):
    return ((z % 4) * 4 + y % 4) * 8 + (x % 4) * 2 + core


def chips():
    return [(z, y, x) for z in range(4) for y in range(4) for x in range(4)]


def swap_cores(v):
    return lax.ppermute(
        v, ("fsdp", "pre"), [(device(*p, c), device(*p, 1 - c)) for p in chips() for c in range(2)]
    )


def from_x(v, d):
    return lax.ppermute(
        v, ("fsdp", "pre"), [(device(z, y, x + d, c), device(z, y, x, c)) for z, y, x in chips() for c in range(2)]
    )


def from_ring(v, phase, d):
    pairs = []
    for z, y, x in chips():
        for c in range(2):
            dz, dy = (0, d) if phase == c else (d, 0)
            pairs.append((device(z + dz, y + dy, x, c), device(z, y, x, c)))
    return lax.ppermute(v, ("fsdp", "pre"), pairs)


def from_ring_across(v, d):
    pairs = []
    for z, y, x in chips():
        for c in range(2):
            dz, dy = (0, d) if c == 0 else (d, 0)
            pairs.append((device(z + dz, y + dy, x, 1 - c), device(z, y, x, c)))
    return lax.ppermute(v, ("fsdp", "pre"), pairs)


def body(inputs, grads_out, owner, offsets, prev_roots):
    slots, _, b, _ = prev_roots.shape
    tokens, cols = grads_out.shape
    half = tokens // 2
    f = lax.axis_index("fsdp").astype(jnp.int32)
    p = lax.axis_index("pre").astype(jnp.int32)
    core = p % 2
    place = jnp.stack([f // 4, f % 4, p // 2, core])
    rows_of = lambda v, c: lax.dynamic_slice_in_dim(v, c * half, half, 0)

    sent = jnp.stack([rows_of(inputs, 1 - core), rows_of(grads_out, 1 - core)])
    recv = swap_cores(sent)
    shard = jnp.stack([rows_of(grads_out, core), recv[1]])

    near = [shard, from_ring(shard, 0, 1), from_ring(shard, 0, 2), from_ring(shard, 0, 3)]
    both = join(near)

    mine = split_features(core.reshape(1), inputs, recv)
    mine = lax.all_to_all(mine, "fsdp", 0, 0, tiled=True)
    both, mine = lax.optimization_barrier((both, mine))
    up = from_ring(both, 1, 1)
    down = from_ring(both, 1, 3)
    a_list = [mine, from_x(mine, 1), from_x(mine, 2), from_x(mine, 3)]
    xb, fourth = fourth_powers(prev_roots.reshape(slots * 2, b, b))
    up, xb, fourth = lax.optimization_barrier((up, xb, fourth))
    xb, fourth = (v.reshape(prev_roots.shape) for v in (xb, fourth))
    own_2 = from_ring(up[:4], 1, 1)
    far_2 = from_ring_across(down[4:], 3)

    share_0, share_1, acc, lhs = first_chunks(place, a_list, [both, up, down])
    pieces = last_chunk(
        place, owner, offsets, lhs, swap_cores(lhs), own_2, far_2, acc, swap_cores(share_0), swap_cores(share_1)
    )
    pieces = lax.all_to_all(pieces, "fsdp", 0, 0, tiled=True)
    return tuple(newton(pieces.reshape(16, slots, -1, b), xb, fourth))


def solution(mesh):
    in_specs = (P("fsdp", "pre"), P("fsdp", "pre"), P(), P(), P(("fsdp", "pre"), None, None, None))
    out_specs = (P(("fsdp", "pre"), None, None), P(("fsdp", "pre"), None, None, None))
    return jax.shard_map(body, mesh=mesh, in_specs=in_specs, out_specs=out_specs, check_vma=False)
```

```python
import jax
import jax.numpy as jnp
from jax import lax
from jax.experimental import pallas as pl
from jax.experimental.pallas import tpu as pltpu
from jax.sharding import PartitionSpec as P

BF = jnp.bfloat16
F32 = jnp.float32
VMEM = 12 * 1024 * 1024
MIDDLE_VMEM = 12 * 1024 * 1024
LARGE_VMEM = 20 * 1024 * 1024
SHORT = pl.CostEstimate(flops=1, bytes_accessed=1, transcendentals=0)


def dot(a, b):
    return jnp.dot(a, b, preferred_element_type=F32)


def params(**kw):
    return pltpu.CompilerParams(vmem_limit_bytes=VMEM, **kw)


def split_kernel(core_ref, a_ref, r_ref, o_ref):
    pieces, rows, tokens = o_ref.shape
    part = rows // 4
    start = pl.multiple_of(core_ref[0] * tokens, tokens)
    for o in range(2):
        flipped = (a_ref[pl.ds(start, tokens), :] if o == 0 else r_ref[0]).T
        for r in range(2):
            for f in range(pieces):
                at, to = (r * pieces + f) * part, (2 * o + r) * part
                o_ref[f, to : to + part, :] = flipped[at : at + part, :]


def split_features(core, a, recv):
    tokens, feats = a.shape
    whole = lambda s: pl.BlockSpec(s, lambda i: (0,) * len(s))
    return pl.pallas_call(
        split_kernel,
        grid=(1,),
        in_specs=[pl.BlockSpec(memory_space=pltpu.SMEM), whole(a.shape), whole((1,) + recv.shape[1:])],
        out_specs=whole((16, feats // 8, tokens // 2)),
        out_shape=jax.ShapeDtypeStruct((16, feats // 8, tokens // 2), BF),
        compiler_params=params(),
        cost_estimate=SHORT,
    )(core, a, recv)


def fourth_kernel(x_ref, xb_ref, f_ref):
    xb = x_ref[0].astype(BF)
    xb_ref[0] = xb
    sq = dot(xb, xb).astype(BF)
    f_ref[0] = (0.25 * dot(sq, sq)).astype(BF)


def fourth_powers(roots):
    n, b, _ = roots.shape
    spec = pl.BlockSpec((1, b, b), lambda i: (i, 0, 0))
    return pl.pallas_call(
        fourth_kernel,
        grid=(n,),
        in_specs=[spec],
        out_specs=[spec, spec],
        out_shape=[pltpu.HBM((n, b, b), BF)] * 2,
        compiler_params=pltpu.CompilerParams(vmem_limit_bytes=MIDDLE_VMEM),
        cost_estimate=SHORT,
    )(roots)


def join_kernel(*refs):
    parts, o_ref = refs[:-1], refs[-1]
    for o in range(2):
        for i, v in enumerate(parts):
            o_ref[o * len(parts) + i] = v[o]


def join(parts):
    n, rows, cols = parts[0].shape
    vmem = pl.BlockSpec(memory_space=pltpu.VMEM)
    return pl.pallas_call(
        join_kernel,
        in_specs=[vmem] * len(parts),
        out_specs=vmem,
        out_shape=jax.ShapeDtypeStruct((n * len(parts), rows, cols), BF),
        compiler_params=params(),
        cost_estimate=SHORT,
    )(*parts)


def token_pieces(place_ref, j):
    z, y, core = place_ref[0], place_ref[1], place_ref[3]
    out = []
    for i in range(4):
        dz = jnp.where(core == 0, j, i)
        dy = jnp.where(core == 0, i, j)
        out.append(lax.rem(z + dz, 4) * 4 + lax.rem(y + dy, 4))
    return out


def left_operand(place_ref, a_refs, j):
    at = token_pieces(place_ref, j)
    rows = [jnp.concatenate([a[f] for f in at], axis=1) for a in a_refs]
    return jnp.concatenate(rows, axis=0)


def product(lhs, *b):
    return dot(lhs, jnp.concatenate([v.reshape(-1, v.shape[-1]) for v in b], axis=0))


def first_kernel(place_ref, *refs):
    a_refs, b_refs, shares, (acc_ref, last_ref) = refs[:4], refs[4:7], refs[7:9], refs[9:]
    lhs = jnp.concatenate([left_operand(place_ref, a_refs, j) for j in (0, 1, 3)], axis=1)
    block = shares[0].shape[1]
    for o in (1, 0):
        for c in range(2):
            at = slice(c * block, (c + 1) * block)
            total = product(lhs, *[v[4 * o : 4 * o + 4, :, at] for v in b_refs])
            if o:
                shares[c][...] = total.astype(BF)
            else:
                acc_ref[:, at] = total
    last_ref[...] = left_operand(place_ref, a_refs, 2)


def first_chunks(place, a_list, chunks):
    n, rows, tokens = a_list[0].shape
    cols = chunks[0].shape[-1]
    full = (4 * rows, 4 * tokens)
    vmem = pl.BlockSpec(memory_space=pltpu.VMEM)
    return pl.pallas_call(
        first_kernel,
        in_specs=[pl.BlockSpec(memory_space=pltpu.SMEM)] + [vmem] * 7,
        out_specs=[vmem] * 4,
        out_shape=[jax.ShapeDtypeStruct(full, BF)] * 2
        + [jax.ShapeDtypeStruct((4 * rows, cols), F32), jax.ShapeDtypeStruct(full, BF)],
        compiler_params=params(),
        cost_estimate=pl.CostEstimate(flops=3 * 2**30, bytes_accessed=12 * 2**20, transcendentals=0),
    )(place, *a_list, *chunks)


def last_kernel(place_ref, owner_ref, offs_ref, lhs_ref, cross_ref, own_ref, far_ref, acc_ref, share_0, share_1, o_ref):
    x, core = place_ref[2], place_ref[3]
    part, block = o_ref.shape[1:]
    o_ref[...] = jnp.zeros_like(o_ref)
    for c in range(2):
        at_cols = slice(c * block, (c + 1) * block)
        total = acc_ref[:, at_cols] + product(lhs_ref[...], own_ref[:, :, at_cols])
        cross = (share_0, share_1)[c][...].astype(F32) + product(cross_ref[...], far_ref[:, :, at_cols])
        col = 2 * (2 * x + core) + c
        for dx in range(4):
            for o in range(2):
                p = 2 * lax.rem(x + dx, 4) + lax.rem(core + o, 2)
                for r in range(2):
                    at = ((dx * 2 + o) * 2 + r) * part
                    to = ((dx * 2 + 1 - o) * 2 + r) * part
                    row = 2 * p + r
                    key = owner_ref[row, col] * 3 + offs_ref[row, col]
                    o_ref[key] = (total[at : at + part] + cross[to : to + part]).astype(BF)


def last_chunk(place, owner, offsets, *operands):
    rows, cols = operands[4].shape
    return pl.pallas_call(
        last_kernel,
        in_specs=[pl.BlockSpec(memory_space=pltpu.SMEM)] * 3
        + [pl.BlockSpec(memory_space=pltpu.VMEM)] * len(operands),
        out_specs=pl.BlockSpec(memory_space=pltpu.VMEM),
        out_shape=jax.ShapeDtypeStruct((48, rows // 16, cols // 2), BF),
        compiler_params=params(),
        cost_estimate=SHORT,
    )(place, owner, offsets, *operands)


def newton_kernel(g_ref, xb_ref, f_ref, u_ref, n_ref):
    size = g_ref.shape[3]
    g = g_ref[...].reshape(size, size)
    gt = g.T
    g32 = g.astype(F32)
    scale = 0.1 / (jnp.sum(g32 * g32) / size + 1e-6)
    stats = [dot(g, gt).astype(BF), dot(gt, g).astype(BF)]
    es = [(scale * dot(f_ref[0, k], stats[k]) + f_ref[0, k].astype(F32)).astype(BF) for k in range(2)]
    squares = [dot(e, e) for e in es]
    f_es = [(1.25 * e.astype(F32) - square).astype(BF) for e, square in zip(es, squares)]
    ts = [(square - 2.5 * e.astype(F32)).astype(BF) for e, square in zip(es, squares)]
    f_es = [(dot(t, v) + 1.5625 * v.astype(F32)).astype(BF) for t, v in zip(ts, f_es)]
    f_es = [dot(t, v) + 1.5625 * v.astype(F32) for t, v in zip(ts, f_es)]
    ws = [(1.25 * e.astype(F32) + v).astype(BF) for e, v in zip(es, f_es)]
    xs = [1.5625 * xb_ref[0, k].astype(F32) - dot(xb_ref[0, k], ws[k]) for k in range(2)]
    for k in range(2):
        n_ref[0, k] = xs[k]
    left, right = (x.astype(BF) for x in xs)
    u_ref[0] = dot(dot(left, g).astype(BF), right).astype(BF)


def newton(pieces, roots, fourth):
    n_src, slots, rows, b = pieces.shape
    pair = pl.BlockSpec((1, 2, b, b), lambda i: (i, 0, 0, 0))
    return pl.pallas_call(
        newton_kernel,
        grid=(slots,),
        in_specs=[pl.BlockSpec((n_src, 1, rows, b), lambda i: (0, i, 0, 0)), pair, pair],
        out_specs=[pl.BlockSpec((1, b, b), lambda i: (i, 0, 0)), pair],
        out_shape=[
            jax.ShapeDtypeStruct((slots, b, b), BF),
            jax.ShapeDtypeStruct((slots, 2, b, b), F32),
        ],
        compiler_params=pltpu.CompilerParams(vmem_limit_bytes=LARGE_VMEM),
        cost_estimate=SHORT,
    )(pieces, roots, fourth)


def device(z, y, x, core):
    return ((z % 4) * 4 + y % 4) * 8 + (x % 4) * 2 + core


def chips():
    return [(z, y, x) for z in range(4) for y in range(4) for x in range(4)]


def swap_cores(v):
    return lax.ppermute(
        v, ("fsdp", "pre"), [(device(*p, c), device(*p, 1 - c)) for p in chips() for c in range(2)]
    )


def from_x(v, d):
    return lax.ppermute(
        v, ("fsdp", "pre"), [(device(z, y, x + d, c), device(z, y, x, c)) for z, y, x in chips() for c in range(2)]
    )


def from_ring(v, phase, d):
    pairs = []
    for z, y, x in chips():
        for c in range(2):
            dz, dy = (0, d) if phase == c else (d, 0)
            pairs.append((device(z + dz, y + dy, x, c), device(z, y, x, c)))
    return lax.ppermute(v, ("fsdp", "pre"), pairs)


def from_ring_across(v, d):
    pairs = []
    for z, y, x in chips():
        for c in range(2):
            dz, dy = (0, d) if c == 0 else (d, 0)
            pairs.append((device(z + dz, y + dy, x, 1 - c), device(z, y, x, c)))
    return lax.ppermute(v, ("fsdp", "pre"), pairs)


def body(inputs, grads_out, owner, offsets, prev_roots):
    slots, _, b, _ = prev_roots.shape
    tokens, cols = grads_out.shape
    half = tokens // 2
    f = lax.axis_index("fsdp").astype(jnp.int32)
    p = lax.axis_index("pre").astype(jnp.int32)
    core = p % 2
    place = jnp.stack([f // 4, f % 4, p // 2, core])
    rows_of = lambda v, c: lax.dynamic_slice_in_dim(v, c * half, half, 0)

    sent = jnp.stack([rows_of(inputs, 1 - core), rows_of(grads_out, 1 - core)])
    recv = swap_cores(sent)
    shard = jnp.stack([rows_of(grads_out, core), recv[1]])

    near = [shard, from_ring(shard, 0, 1), from_ring(shard, 0, 2), from_ring(shard, 0, 3)]
    both = join(near)

    mine = split_features(core.reshape(1), inputs, recv)
    mine = lax.all_to_all(mine, "fsdp", 0, 0, tiled=True)
    both, mine = lax.optimization_barrier((both, mine))
    up = from_ring(both, 1, 1)
    down = from_ring(both, 1, 3)
    a_list = [mine, from_x(mine, 1), from_x(mine, 2), from_x(mine, 3)]
    xb, fourth = fourth_powers(prev_roots.reshape(slots * 2, b, b))
    up, xb, fourth = lax.optimization_barrier((up, xb, fourth))
    xb, fourth = (v.reshape(prev_roots.shape) for v in (xb, fourth))
    own_2 = from_ring(up[:4], 1, 1)
    far_2 = from_ring_across(down[4:], 3)

    share_0, share_1, acc, lhs = first_chunks(place, a_list, [both, up, down])
    pieces = last_chunk(
        place, owner, offsets, lhs, swap_cores(lhs), own_2, far_2, acc, swap_cores(share_0), swap_cores(share_1)
    )
    pieces = lax.all_to_all(pieces, "fsdp", 0, 0, tiled=True)
    return tuple(newton(pieces.reshape(16, slots, -1, b), xb, fourth))


def solution(mesh):
    in_specs = (P("fsdp", "pre"), P("fsdp", "pre"), P(), P(), P(("fsdp", "pre"), None, None, None))
    out_specs = (P(("fsdp", "pre"), None, None), P(("fsdp", "pre"), None, None, None))
    return jax.shard_map(body, mesh=mesh, in_specs=in_specs, out_specs=out_specs, check_vma=False)
```

```python
import jax
import jax.numpy as jnp
from jax import lax
from jax.experimental import pallas as pl
from jax.experimental.pallas import tpu as pltpu
from jax.sharding import PartitionSpec as P

BF = jnp.bfloat16
F32 = jnp.float32
VMEM = 12 * 1024 * 1024
MIDDLE_VMEM = 12 * 1024 * 1024
LARGE_VMEM = 20 * 1024 * 1024
SHORT = pl.CostEstimate(flops=1, bytes_accessed=1, transcendentals=0)


def dot(a, b):
    return jnp.dot(a, b, preferred_element_type=F32)


def params(**kw):
    return pltpu.CompilerParams(vmem_limit_bytes=VMEM, **kw)


def split_kernel(place_ref, a_ref, r_ref, o_ref):
    pieces, rows, tokens = o_ref.shape
    part = rows // 4
    start = pl.multiple_of(place_ref[3] * tokens, tokens)
    for o in range(2):
        flipped = (a_ref[pl.ds(start, tokens), :] if o == 0 else r_ref[0]).T
        for r in range(2):
            for f in range(pieces):
                at, to = (r * pieces + f) * part, (2 * o + r) * part
                o_ref[f, to : to + part, :] = flipped[at : at + part, :]


def split_features(place, a, recv):
    tokens, feats = a.shape
    whole = lambda s: pl.BlockSpec(s, lambda i: (0,) * len(s))
    return pl.pallas_call(
        split_kernel,
        grid=(1,),
        in_specs=[pl.BlockSpec(memory_space=pltpu.SMEM), whole(a.shape), whole((1,) + recv.shape[1:])],
        out_specs=whole((16, feats // 8, tokens // 2)),
        out_shape=jax.ShapeDtypeStruct((16, feats // 8, tokens // 2), BF),
        compiler_params=params(),
        cost_estimate=SHORT,
    )(place, a, recv)


def fourth_kernel(x_ref, xb_ref, f_ref):
    xb = x_ref[0].astype(BF)
    xb_ref[0] = xb
    sq = dot(xb, xb).astype(BF)
    f_ref[0] = (0.25 * dot(sq, sq)).astype(BF)


def fourth_powers(roots):
    n, b, _ = roots.shape
    spec = pl.BlockSpec((1, b, b), lambda i: (i, 0, 0))
    return pl.pallas_call(
        fourth_kernel,
        grid=(n,),
        in_specs=[spec],
        out_specs=[spec, spec],
        out_shape=[pltpu.HBM((n, b, b), BF)] * 2,
        compiler_params=pltpu.CompilerParams(vmem_limit_bytes=MIDDLE_VMEM),
        cost_estimate=SHORT,
    )(roots)


def copy_kernel(v_ref, o_ref):
    o_ref[...] = v_ref[...]


def to_vmem(v):
    vmem = pl.BlockSpec(memory_space=pltpu.VMEM)
    return pl.pallas_call(
        copy_kernel,
        in_specs=[vmem],
        out_specs=vmem,
        out_shape=jax.ShapeDtypeStruct(v.shape, v.dtype),
        compiler_params=params(),
        cost_estimate=SHORT,
    )(v)


def join_kernel(*refs):
    parts, o_ref = refs[:-1], refs[-1]
    for o in range(2):
        for i, v in enumerate(parts):
            o_ref[o * len(parts) + i] = v[o]


def join(parts):
    n, rows, cols = parts[0].shape
    vmem = pl.BlockSpec(memory_space=pltpu.VMEM)
    return pl.pallas_call(
        join_kernel,
        in_specs=[vmem] * len(parts),
        out_specs=vmem,
        out_shape=jax.ShapeDtypeStruct((n * len(parts), rows, cols), BF),
        compiler_params=params(),
        cost_estimate=SHORT,
    )(*parts)


def token_pieces(place_ref, j):
    z, y, core = place_ref[0], place_ref[1], place_ref[3]
    out = []
    for i in range(4):
        dz = jnp.where(core == 0, j, i)
        dy = jnp.where(core == 0, i, j)
        out.append(lax.rem(z + dz, 4) * 4 + lax.rem(y + dy, 4))
    return out


def left_operand(place_ref, a_refs, j):
    at = token_pieces(place_ref, j)
    rows = [jnp.concatenate([a[f] for f in at], axis=1) for a in a_refs]
    return jnp.concatenate(rows, axis=0)


def product(lhs, *b):
    return dot(lhs, jnp.concatenate([v.reshape(-1, v.shape[-1]) for v in b], axis=0))


def first_kernel(place_ref, *refs):
    a_refs, b_refs, shares, (acc_ref, last_ref) = refs[:4], refs[4:7], refs[7:9], refs[9:]
    lhs = jnp.concatenate([left_operand(place_ref, a_refs, j) for j in (0, 1, 3)], axis=1)
    block = shares[0].shape[1]
    for o in (1, 0):
        for c in range(2):
            at = slice(c * block, (c + 1) * block)
            total = product(lhs, *[v[4 * o : 4 * o + 4, :, at] for v in b_refs])
            if o:
                shares[c][...] = total.astype(BF)
            else:
                acc_ref[:, at] = total
    last_ref[...] = left_operand(place_ref, a_refs, 2)


def first_chunks(place, a_list, chunks):
    n, rows, tokens = a_list[0].shape
    cols = chunks[0].shape[-1]
    full = (4 * rows, 4 * tokens)
    vmem = pl.BlockSpec(memory_space=pltpu.VMEM)
    return pl.pallas_call(
        first_kernel,
        in_specs=[pl.BlockSpec(memory_space=pltpu.SMEM)] + [vmem] * 7,
        out_specs=[vmem] * 4,
        out_shape=[jax.ShapeDtypeStruct(full, BF)] * 2
        + [jax.ShapeDtypeStruct((4 * rows, cols), F32), jax.ShapeDtypeStruct(full, BF)],
        compiler_params=params(),
        cost_estimate=pl.CostEstimate(flops=3 * 2**30, bytes_accessed=12 * 2**20, transcendentals=0),
    )(place, *a_list, *chunks)


def last_kernel(place_ref, owner_ref, offs_ref, lhs_ref, cross_ref, own_ref, far_ref, acc_ref, share_0, share_1, o_ref):
    x, core = place_ref[2], place_ref[3]
    part, block = o_ref.shape[1:]
    o_ref[...] = jnp.zeros_like(o_ref)
    for c in range(2):
        at_cols = slice(c * block, (c + 1) * block)
        total = acc_ref[:, at_cols] + product(lhs_ref[...], own_ref[:, :, at_cols])
        cross = (share_0, share_1)[c][...].astype(F32) + product(cross_ref[...], far_ref[:, :, at_cols])
        col = 2 * (2 * x + core) + c
        for dx in range(4):
            for o in range(2):
                p = 2 * lax.rem(x + dx, 4) + lax.rem(core + o, 2)
                for r in range(2):
                    at = ((dx * 2 + o) * 2 + r) * part
                    to = ((dx * 2 + 1 - o) * 2 + r) * part
                    row = 2 * p + r
                    key = owner_ref[row, col] * 3 + offs_ref[row, col]
                    o_ref[key] = (total[at : at + part] + cross[to : to + part]).astype(BF)


def last_chunk(place, owner, offsets, *operands):
    rows, cols = operands[4].shape
    return pl.pallas_call(
        last_kernel,
        in_specs=[pl.BlockSpec(memory_space=pltpu.SMEM)] * 3
        + [pl.BlockSpec(memory_space=pltpu.VMEM)] * len(operands),
        out_specs=pl.BlockSpec(memory_space=pltpu.VMEM),
        out_shape=jax.ShapeDtypeStruct((48, rows // 16, cols // 2), BF),
        compiler_params=params(),
        cost_estimate=SHORT,
    )(place, owner, offsets, *operands)


def newton_kernel(g_ref, xb_ref, f_ref, u_ref, n_ref):
    size = g_ref.shape[3]
    g = g_ref[...].reshape(size, size)
    gt = g.T
    g32 = g.astype(F32)
    scale = 0.1 / (jnp.sum(g32 * g32) / size + 1e-6)
    stats = [dot(g, gt).astype(BF), dot(gt, g).astype(BF)]
    es = [(scale * dot(f_ref[0, k], stats[k]) + f_ref[0, k].astype(F32)).astype(BF) for k in range(2)]
    squares = [dot(e, e) for e in es]
    f_es = [(1.25 * e.astype(F32) - square).astype(BF) for e, square in zip(es, squares)]
    ts = [(square - 2.5 * e.astype(F32)).astype(BF) for e, square in zip(es, squares)]
    f_es = [(dot(t, v) + 1.5625 * v.astype(F32)).astype(BF) for t, v in zip(ts, f_es)]
    f_es = [dot(t, v) + 1.5625 * v.astype(F32) for t, v in zip(ts, f_es)]
    ws = [(1.25 * e.astype(F32) + v).astype(BF) for e, v in zip(es, f_es)]
    xs = [1.5625 * xb_ref[0, k].astype(F32) - dot(xb_ref[0, k], ws[k]) for k in range(2)]
    for k in range(2):
        n_ref[0, k] = xs[k]
    left, right = (x.astype(BF) for x in xs)
    u_ref[0] = dot(dot(left, g).astype(BF), right).astype(BF)


def newton(pieces, roots, fourth):
    n_src, slots, rows, b = pieces.shape
    pair = pl.BlockSpec((1, 2, b, b), lambda i: (i, 0, 0, 0))
    return pl.pallas_call(
        newton_kernel,
        grid=(slots,),
        in_specs=[pl.BlockSpec((n_src, 1, rows, b), lambda i: (0, i, 0, 0)), pair, pair],
        out_specs=[pl.BlockSpec((1, b, b), lambda i: (i, 0, 0)), pair],
        out_shape=[
            jax.ShapeDtypeStruct((slots, b, b), BF),
            jax.ShapeDtypeStruct((slots, 2, b, b), F32),
        ],
        compiler_params=pltpu.CompilerParams(vmem_limit_bytes=LARGE_VMEM),
        cost_estimate=SHORT,
    )(pieces, roots, fourth)


def device(z, y, x, core):
    return ((z % 4) * 4 + y % 4) * 8 + (x % 4) * 2 + core


def chips():
    return [(z, y, x) for z in range(4) for y in range(4) for x in range(4)]


def swap_cores(v):
    return lax.ppermute(
        v, ("fsdp", "pre"), [(device(*p, c), device(*p, 1 - c)) for p in chips() for c in range(2)]
    )


def from_x(v, d):
    return lax.ppermute(
        v, ("fsdp", "pre"), [(device(z, y, x + d, c), device(z, y, x, c)) for z, y, x in chips() for c in range(2)]
    )


def from_ring(v, phase, d):
    pairs = []
    for z, y, x in chips():
        for c in range(2):
            dz, dy = (0, d) if phase == c else (d, 0)
            pairs.append((device(z + dz, y + dy, x, c), device(z, y, x, c)))
    return lax.ppermute(v, ("fsdp", "pre"), pairs)


def from_ring_across(v, d):
    pairs = []
    for z, y, x in chips():
        for c in range(2):
            dz, dy = (0, d) if c == 0 else (d, 0)
            pairs.append((device(z + dz, y + dy, x, 1 - c), device(z, y, x, c)))
    return lax.ppermute(v, ("fsdp", "pre"), pairs)


def body(inputs, grads_out, owner, offsets, prev_roots):
    slots, _, b, _ = prev_roots.shape
    tokens, cols = grads_out.shape
    half = tokens // 2
    f = lax.axis_index("fsdp").astype(jnp.int32)
    p = lax.axis_index("pre").astype(jnp.int32)
    core = p % 2
    place = jnp.stack([f // 4, f % 4, p // 2, core])
    rows_of = lambda v, c: lax.dynamic_slice_in_dim(v, c * half, half, 0)

    sent = jnp.stack([rows_of(inputs, 1 - core), rows_of(grads_out, 1 - core)])
    recv = swap_cores(sent)
    shard = jnp.stack([rows_of(grads_out, core), recv[1]])

    near = [shard, from_ring(shard, 0, 1), from_ring(shard, 0, 2), from_ring(shard, 0, 3)]
    both = join(near)

    mine = split_features(place, inputs, recv)
    mine = lax.all_to_all(mine, "fsdp", 0, 0, tiled=True)
    both, mine = lax.optimization_barrier((both, mine))
    up = from_ring(both, 1, 1)
    down = from_ring(both, 1, 3)
    mine = to_vmem(mine)
    a_list = [mine, from_x(mine, 1), from_x(mine, 2), from_x(mine, 3)]
    xb, fourth = fourth_powers(prev_roots.reshape(slots * 2, b, b))
    up, xb, fourth = lax.optimization_barrier((up, xb, fourth))
    xb, fourth = (v.reshape(prev_roots.shape) for v in (xb, fourth))
    own_2 = from_ring(up[:4], 1, 1)
    far_2 = from_ring_across(down[4:], 3)

    share_0, share_1, acc, lhs = first_chunks(place, a_list, [both, up, down])
    pieces = last_chunk(
        place, owner, offsets, lhs, swap_cores(lhs), own_2, far_2, acc, swap_cores(share_0), swap_cores(share_1)
    )
    pieces = lax.all_to_all(pieces, "fsdp", 0, 0, tiled=True)
    return tuple(newton(pieces.reshape(16, slots, -1, b), xb, fourth))


def solution(mesh):
    in_specs = (P("fsdp", "pre"), P("fsdp", "pre"), P(), P(), P(("fsdp", "pre"), None, None, None))
    out_specs = (P(("fsdp", "pre"), None, None), P(("fsdp", "pre"), None, None, None))
    return jax.shard_map(body, mesh=mesh, in_specs=in_specs, out_specs=out_specs, check_vma=False)
```

```python
import jax
import jax.numpy as jnp
from jax import lax
from jax.experimental import pallas as pl
from jax.experimental.pallas import tpu as pltpu
from jax.sharding import PartitionSpec as P

BF = jnp.bfloat16
F32 = jnp.float32
VMEM = 12 * 1024 * 1024
MIDDLE_VMEM = 12 * 1024 * 1024
LARGE_VMEM = 20 * 1024 * 1024
SHORT = pl.CostEstimate(flops=1, bytes_accessed=1, transcendentals=0)


def dot(a, b):
    return jnp.dot(a, b, preferred_element_type=F32)


def params(**kw):
    return pltpu.CompilerParams(vmem_limit_bytes=VMEM, **kw)


def split_kernel(place_ref, a_ref, r_ref, o_ref):
    pieces, rows, tokens = o_ref.shape
    part = rows // 4
    start = pl.multiple_of(place_ref[3] * tokens, tokens)
    for o in range(2):
        flipped = (a_ref[pl.ds(start, tokens), :] if o == 0 else r_ref[0]).T
        for r in range(2):
            for f in range(pieces):
                at, to = (r * pieces + f) * part, (2 * o + r) * part
                o_ref[f, to : to + part, :] = flipped[at : at + part, :]


def split_features(place, a, recv):
    tokens, feats = a.shape
    whole = lambda s: pl.BlockSpec(s, lambda i: (0,) * len(s))
    return pl.pallas_call(
        split_kernel,
        grid=(1,),
        in_specs=[pl.BlockSpec(memory_space=pltpu.SMEM), whole(a.shape), whole((1,) + recv.shape[1:])],
        out_specs=whole((16, feats // 8, tokens // 2)),
        out_shape=jax.ShapeDtypeStruct((16, feats // 8, tokens // 2), BF),
        compiler_params=params(),
        cost_estimate=SHORT,
    )(place, a, recv)


def fourth_kernel(x_ref, xb_ref, f_ref):
    xb = x_ref[0].astype(BF)
    xb_ref[0] = xb
    sq = dot(xb, xb).astype(BF)
    f_ref[0] = (0.25 * dot(sq, sq)).astype(BF)


def fourth_powers(roots):
    n, b, _ = roots.shape
    spec = pl.BlockSpec((1, b, b), lambda i: (i, 0, 0))
    return pl.pallas_call(
        fourth_kernel,
        grid=(n,),
        in_specs=[spec],
        out_specs=[spec, spec],
        out_shape=[pltpu.HBM((n, b, b), BF)] * 2,
        compiler_params=pltpu.CompilerParams(vmem_limit_bytes=MIDDLE_VMEM),
        cost_estimate=SHORT,
    )(roots)


def copy_kernel(v_ref, o_ref):
    o_ref[...] = v_ref[...]


def to_vmem(v):
    vmem = pl.BlockSpec(memory_space=pltpu.VMEM)
    return pl.pallas_call(
        copy_kernel,
        in_specs=[vmem],
        out_specs=vmem,
        out_shape=jax.ShapeDtypeStruct(v.shape, v.dtype),
        compiler_params=params(),
        cost_estimate=SHORT,
    )(v)


def join_kernel(*refs):
    for o, o_ref in enumerate(refs[-2:]):
        for i, v in enumerate(refs[:-2]):
            o_ref[i] = v[o]


def join(parts):
    n, rows, cols = parts[0].shape
    vmem = pl.BlockSpec(memory_space=pltpu.VMEM)
    return pl.pallas_call(
        join_kernel,
        in_specs=[vmem] * len(parts),
        out_specs=[vmem] * n,
        out_shape=[jax.ShapeDtypeStruct((len(parts), rows, cols), BF)] * n,
        compiler_params=params(),
        cost_estimate=SHORT,
    )(*parts)


def token_pieces(place_ref, j):
    z, y, core = place_ref[0], place_ref[1], place_ref[3]
    out = []
    for i in range(4):
        dz = jnp.where(core == 0, j, i)
        dy = jnp.where(core == 0, i, j)
        out.append(lax.rem(z + dz, 4) * 4 + lax.rem(y + dy, 4))
    return out


def left_operand(place_ref, a_refs, j):
    at = token_pieces(place_ref, j)
    rows = [jnp.concatenate([a[f] for f in at], axis=1) for a in a_refs]
    return jnp.concatenate(rows, axis=0)


def product(lhs, *b):
    return dot(lhs, jnp.concatenate([v.reshape(-1, v.shape[-1]) for v in b], axis=0))


def first_kernel(place_ref, *refs):
    a_refs, b_refs, shares, (acc_ref, last_ref) = refs[:4], refs[4:10], refs[10:12], refs[12:]
    lhs = jnp.concatenate([left_operand(place_ref, a_refs, j) for j in (0, 1, 3)], axis=1)
    block = shares[0].shape[1]
    for o in (1, 0):
        for c in range(2):
            at = slice(c * block, (c + 1) * block)
            total = product(lhs, *[v[:, :, at] for v in b_refs[o::2]])
            if o:
                shares[c][...] = total.astype(BF)
            else:
                acc_ref[:, at] = total
    last_ref[...] = left_operand(place_ref, a_refs, 2)


def first_chunks(place, a_list, chunks):
    n, rows, tokens = a_list[0].shape
    cols = chunks[0].shape[-1]
    full = (4 * rows, 4 * tokens)
    vmem = pl.BlockSpec(memory_space=pltpu.VMEM)
    return pl.pallas_call(
        first_kernel,
        in_specs=[pl.BlockSpec(memory_space=pltpu.SMEM)] + [vmem] * 10,
        out_specs=[vmem] * 4,
        out_shape=[jax.ShapeDtypeStruct(full, BF)] * 2
        + [jax.ShapeDtypeStruct((4 * rows, cols), F32), jax.ShapeDtypeStruct(full, BF)],
        compiler_params=params(),
        cost_estimate=pl.CostEstimate(flops=3 * 2**30, bytes_accessed=12 * 2**20, transcendentals=0),
    )(place, *a_list, *chunks)


def last_kernel(place_ref, owner_ref, offs_ref, lhs_ref, cross_ref, own_ref, far_ref, acc_ref, share_0, share_1, o_ref):
    x, core = place_ref[2], place_ref[3]
    part, block = o_ref.shape[1:]
    o_ref[...] = jnp.zeros_like(o_ref)
    for c in range(2):
        at_cols = slice(c * block, (c + 1) * block)
        total = acc_ref[:, at_cols] + product(lhs_ref[...], own_ref[:, :, at_cols])
        cross = (share_0, share_1)[c][...].astype(F32) + product(cross_ref[...], far_ref[:, :, at_cols])
        col = 2 * (2 * x + core) + c
        for dx in range(4):
            for o in range(2):
                p = 2 * lax.rem(x + dx, 4) + lax.rem(core + o, 2)
                for r in range(2):
                    at = ((dx * 2 + o) * 2 + r) * part
                    to = ((dx * 2 + 1 - o) * 2 + r) * part
                    row = 2 * p + r
                    key = owner_ref[row, col] * 3 + offs_ref[row, col]
                    o_ref[key] = (total[at : at + part] + cross[to : to + part]).astype(BF)


def last_chunk(place, owner, offsets, *operands):
    rows, cols = operands[4].shape
    return pl.pallas_call(
        last_kernel,
        in_specs=[pl.BlockSpec(memory_space=pltpu.SMEM)] * 3
        + [pl.BlockSpec(memory_space=pltpu.VMEM)] * len(operands),
        out_specs=pl.BlockSpec(memory_space=pltpu.VMEM),
        out_shape=jax.ShapeDtypeStruct((48, rows // 16, cols // 2), BF),
        compiler_params=params(),
        cost_estimate=SHORT,
    )(place, owner, offsets, *operands)


def newton_kernel(g_ref, xb_ref, f_ref, u_ref, n_ref):
    size = g_ref.shape[3]
    g = g_ref[...].reshape(size, size)
    gt = g.T
    g32 = g.astype(F32)
    scale = 0.1 / (jnp.sum(g32 * g32) / size + 1e-6)
    stats = [dot(g, gt).astype(BF), dot(gt, g).astype(BF)]
    es = [(scale * dot(f_ref[0, k], stats[k]) + f_ref[0, k].astype(F32)).astype(BF) for k in range(2)]
    squares = [dot(e, e) for e in es]
    f_es = [(1.25 * e.astype(F32) - square).astype(BF) for e, square in zip(es, squares)]
    ts = [(square - 2.5 * e.astype(F32)).astype(BF) for e, square in zip(es, squares)]
    f_es = [(dot(t, v) + 1.5625 * v.astype(F32)).astype(BF) for t, v in zip(ts, f_es)]
    f_es = [dot(t, v) + 1.5625 * v.astype(F32) for t, v in zip(ts, f_es)]
    ws = [(1.25 * e.astype(F32) + v).astype(BF) for e, v in zip(es, f_es)]
    xs = [1.5625 * xb_ref[0, k].astype(F32) - dot(xb_ref[0, k], ws[k]) for k in range(2)]
    for k in range(2):
        n_ref[0, k] = xs[k]
    left, right = (x.astype(BF) for x in xs)
    u_ref[0] = dot(dot(left, g).astype(BF), right).astype(BF)


def newton(pieces, roots, fourth):
    n_src, slots, rows, b = pieces.shape
    pair = pl.BlockSpec((1, 2, b, b), lambda i: (i, 0, 0, 0))
    return pl.pallas_call(
        newton_kernel,
        grid=(slots,),
        in_specs=[pl.BlockSpec((n_src, 1, rows, b), lambda i: (0, i, 0, 0)), pair, pair],
        out_specs=[pl.BlockSpec((1, b, b), lambda i: (i, 0, 0)), pair],
        out_shape=[
            jax.ShapeDtypeStruct((slots, b, b), BF),
            jax.ShapeDtypeStruct((slots, 2, b, b), F32),
        ],
        compiler_params=pltpu.CompilerParams(vmem_limit_bytes=LARGE_VMEM),
        cost_estimate=SHORT,
    )(pieces, roots, fourth)


def device(z, y, x, core):
    return ((z % 4) * 4 + y % 4) * 8 + (x % 4) * 2 + core


def chips():
    return [(z, y, x) for z in range(4) for y in range(4) for x in range(4)]


def swap_cores(v):
    return lax.ppermute(
        v, ("fsdp", "pre"), [(device(*p, c), device(*p, 1 - c)) for p in chips() for c in range(2)]
    )


def from_x(v, d):
    return lax.ppermute(
        v, ("fsdp", "pre"), [(device(z, y, x + d, c), device(z, y, x, c)) for z, y, x in chips() for c in range(2)]
    )


def from_ring(v, phase, d):
    pairs = []
    for z, y, x in chips():
        for c in range(2):
            dz, dy = (0, d) if phase == c else (d, 0)
            pairs.append((device(z + dz, y + dy, x, c), device(z, y, x, c)))
    return lax.ppermute(v, ("fsdp", "pre"), pairs)


def from_ring_across(v, d):
    pairs = []
    for z, y, x in chips():
        for c in range(2):
            dz, dy = (0, d) if c == 0 else (d, 0)
            pairs.append((device(z + dz, y + dy, x, 1 - c), device(z, y, x, c)))
    return lax.ppermute(v, ("fsdp", "pre"), pairs)


def body(inputs, grads_out, owner, offsets, prev_roots):
    slots, _, b, _ = prev_roots.shape
    tokens, cols = grads_out.shape
    half = tokens // 2
    f = lax.axis_index("fsdp").astype(jnp.int32)
    p = lax.axis_index("pre").astype(jnp.int32)
    core = p % 2
    place = jnp.stack([f // 4, f % 4, p // 2, core])
    rows_of = lambda v, c: lax.dynamic_slice_in_dim(v, c * half, half, 0)

    sent = jnp.stack([rows_of(inputs, 1 - core), rows_of(grads_out, 1 - core)])
    recv = swap_cores(sent)
    shard = jnp.stack([rows_of(grads_out, core), recv[1]])

    near = [shard, from_ring(shard, 0, 1), from_ring(shard, 0, 2), from_ring(shard, 0, 3)]
    own, other = join(near)

    mine = split_features(place, inputs, recv)
    mine = lax.all_to_all(mine, "fsdp", 0, 0, tiled=True)
    own, other, mine = lax.optimization_barrier((own, other, mine))
    mine = to_vmem(mine)
    own_1, other_3 = from_ring(own, 1, 1), from_ring(other, 1, 3)
    next_x, last_x = from_x(mine, 1), from_x(mine, 3)
    far_x = from_x(mine, 2)
    own_t, other_t, next_x, last_x = lax.optimization_barrier((own, other, next_x, last_x))
    other_1, own_3 = from_ring(other_t, 1, 1), from_ring(own_t, 1, 3)
    xb, fourth = fourth_powers(prev_roots.reshape(slots * 2, b, b))
    other_1, xb, fourth = lax.optimization_barrier((other_1, xb, fourth))
    xb, fourth = (v.reshape(prev_roots.shape) for v in (xb, fourth))
    own_2 = from_ring(own_1, 1, 1)
    far_2 = from_ring_across(other_3, 3)

    chunks = [own, other, own_1, other_1, own_3, other_3]
    share_0, share_1, acc, lhs = first_chunks(place, [mine, next_x, far_x, last_x], chunks)
    pieces = last_chunk(
        place, owner, offsets, lhs, swap_cores(lhs), own_2, far_2, acc, swap_cores(share_0), swap_cores(share_1)
    )
    pieces = lax.all_to_all(pieces, "fsdp", 0, 0, tiled=True)
    return tuple(newton(pieces.reshape(16, slots, -1, b), xb, fourth))


def solution(mesh):
    in_specs = (P("fsdp", "pre"), P("fsdp", "pre"), P(), P(), P(("fsdp", "pre"), None, None, None))
    out_specs = (P(("fsdp", "pre"), None, None), P(("fsdp", "pre"), None, None, None))
    return jax.shard_map(body, mesh=mesh, in_specs=in_specs, out_specs=out_specs, check_vma=False)
```

```python
import jax
import jax.numpy as jnp
from jax import lax
from jax.experimental import pallas as pl
from jax.experimental.pallas import tpu as pltpu
from jax.sharding import PartitionSpec as P

BF = jnp.bfloat16
F32 = jnp.float32
VMEM = 12 * 1024 * 1024
MIDDLE_VMEM = 12 * 1024 * 1024
LARGE_VMEM = 20 * 1024 * 1024
SHORT = pl.CostEstimate(flops=1, bytes_accessed=1, transcendentals=0)


def dot(a, b):
    return jnp.dot(a, b, preferred_element_type=F32)


def params(**kw):
    return pltpu.CompilerParams(vmem_limit_bytes=VMEM, **kw)


def split_kernel(place_ref, a_ref, r_ref, o_ref):
    pieces, rows, tokens = o_ref.shape
    part = rows // 4
    start = pl.multiple_of(place_ref[3] * tokens, tokens)
    for o in range(2):
        flipped = (a_ref[pl.ds(start, tokens), :] if o == 0 else r_ref[0]).T
        for r in range(2):
            for f in range(pieces):
                at, to = (r * pieces + f) * part, (2 * o + r) * part
                o_ref[f, to : to + part, :] = flipped[at : at + part, :]


def split_features(place, a, recv):
    tokens, feats = a.shape
    whole = lambda s: pl.BlockSpec(s, lambda i: (0,) * len(s))
    return pl.pallas_call(
        split_kernel,
        grid=(1,),
        in_specs=[pl.BlockSpec(memory_space=pltpu.SMEM), whole(a.shape), whole((1,) + recv.shape[1:])],
        out_specs=whole((16, feats // 8, tokens // 2)),
        out_shape=jax.ShapeDtypeStruct((16, feats // 8, tokens // 2), BF),
        compiler_params=params(),
        cost_estimate=SHORT,
    )(place, a, recv)


def fourth_kernel(x_ref, xb_ref, f_ref):
    xb = x_ref[0].astype(BF)
    xb_ref[0] = xb
    sq = dot(xb, xb).astype(BF)
    f_ref[0] = (0.25 * dot(sq, sq)).astype(BF)


def fourth_powers(roots):
    n, b, _ = roots.shape
    spec = pl.BlockSpec((1, b, b), lambda i: (i, 0, 0))
    return pl.pallas_call(
        fourth_kernel,
        grid=(n,),
        in_specs=[spec],
        out_specs=[spec, spec],
        out_shape=[jax.ShapeDtypeStruct((n, b, b), BF)] * 2,
        compiler_params=pltpu.CompilerParams(vmem_limit_bytes=MIDDLE_VMEM),
        cost_estimate=SHORT,
    )(roots)


def copy_kernel(v_ref, o_ref):
    o_ref[...] = v_ref[...]


def to_vmem(v):
    vmem = pl.BlockSpec(memory_space=pltpu.VMEM)
    return pl.pallas_call(
        copy_kernel,
        in_specs=[vmem],
        out_specs=vmem,
        out_shape=jax.ShapeDtypeStruct(v.shape, v.dtype),
        compiler_params=params(),
        cost_estimate=SHORT,
    )(v)


def join_kernel(*refs):
    for o, o_ref in enumerate(refs[-2:]):
        for i, v in enumerate(refs[:-2]):
            o_ref[i] = v[o]


def join(parts):
    n, rows, cols = parts[0].shape
    vmem = pl.BlockSpec(memory_space=pltpu.VMEM)
    return pl.pallas_call(
        join_kernel,
        in_specs=[vmem] * len(parts),
        out_specs=[vmem] * n,
        out_shape=[jax.ShapeDtypeStruct((len(parts), rows, cols), BF)] * n,
        compiler_params=params(),
        cost_estimate=SHORT,
    )(*parts)


def token_pieces(place_ref, j):
    z, y, core = place_ref[0], place_ref[1], place_ref[3]
    out = []
    for i in range(4):
        dz = jnp.where(core == 0, j, i)
        dy = jnp.where(core == 0, i, j)
        out.append(lax.rem(z + dz, 4) * 4 + lax.rem(y + dy, 4))
    return out


def left_operand(place_ref, a_refs, j):
    at = token_pieces(place_ref, j)
    rows = [jnp.concatenate([a[f] for f in at], axis=1) for a in a_refs]
    return jnp.concatenate(rows, axis=0)


def product(lhs, *b):
    return dot(lhs, jnp.concatenate([v.reshape(-1, v.shape[-1]) for v in b], axis=0))


def first_kernel(place_ref, *refs):
    a_refs, b_refs, shares, (acc_ref, last_ref) = refs[:4], refs[4:10], refs[10:12], refs[12:]
    lhs = jnp.concatenate([left_operand(place_ref, a_refs, j) for j in (0, 1, 3)], axis=1)
    block = shares[0].shape[1]
    for o in (1, 0):
        for c in range(2):
            at = slice(c * block, (c + 1) * block)
            total = product(lhs, *[v[:, :, at] for v in b_refs[o::2]])
            if o:
                shares[c][...] = total.astype(BF)
            else:
                acc_ref[:, at] = total
    last_ref[...] = left_operand(place_ref, a_refs, 2)


def first_chunks(place, a_list, chunks):
    n, rows, tokens = a_list[0].shape
    cols = chunks[0].shape[-1]
    full = (4 * rows, 4 * tokens)
    vmem = pl.BlockSpec(memory_space=pltpu.VMEM)
    return pl.pallas_call(
        first_kernel,
        in_specs=[pl.BlockSpec(memory_space=pltpu.SMEM)] + [vmem] * 10,
        out_specs=[vmem] * 4,
        out_shape=[jax.ShapeDtypeStruct(full, BF)] * 2
        + [jax.ShapeDtypeStruct((4 * rows, cols), F32), jax.ShapeDtypeStruct(full, BF)],
        compiler_params=params(),
        cost_estimate=pl.CostEstimate(flops=3 * 2**30, bytes_accessed=12 * 2**20, transcendentals=0),
    )(place, *a_list, *chunks)


def last_kernel(place_ref, owner_ref, offs_ref, lhs_ref, cross_ref, own_ref, far_ref, acc_ref, share_0, share_1, o_ref):
    x, core = place_ref[2], place_ref[3]
    part, block = o_ref.shape[1:]
    o_ref[...] = jnp.zeros_like(o_ref)
    for c in range(2):
        at_cols = slice(c * block, (c + 1) * block)
        total = acc_ref[:, at_cols] + product(lhs_ref[...], own_ref[:, :, at_cols])
        cross = (share_0, share_1)[c][...].astype(F32) + product(cross_ref[...], far_ref[:, :, at_cols])
        col = 2 * (2 * x + core) + c
        for dx in range(4):
            for o in range(2):
                p = 2 * lax.rem(x + dx, 4) + lax.rem(core + o, 2)
                for r in range(2):
                    at = ((dx * 2 + o) * 2 + r) * part
                    to = ((dx * 2 + 1 - o) * 2 + r) * part
                    row = 2 * p + r
                    key = owner_ref[row, col] * 3 + offs_ref[row, col]
                    o_ref[key] = (total[at : at + part] + cross[to : to + part]).astype(BF)


def last_chunk(place, owner, offsets, *operands):
    rows, cols = operands[4].shape
    return pl.pallas_call(
        last_kernel,
        in_specs=[pl.BlockSpec(memory_space=pltpu.SMEM)] * 3
        + [pl.BlockSpec(memory_space=pltpu.VMEM)] * len(operands),
        out_specs=pl.BlockSpec(memory_space=pltpu.VMEM),
        out_shape=jax.ShapeDtypeStruct((48, rows // 16, cols // 2), BF),
        compiler_params=params(),
        cost_estimate=SHORT,
    )(place, owner, offsets, *operands)


def newton_kernel(g_ref, xb_ref, f_ref, u_ref, n_ref):
    size = g_ref.shape[3]
    slot = pl.program_id(0)
    g = g_ref[...].reshape(size, size)
    gt = g.T
    g32 = g.astype(F32)
    scale = 0.1 / (jnp.sum(g32 * g32) / size + 1e-6)
    stats = [dot(g, gt).astype(BF), dot(gt, g).astype(BF)]
    es = [(scale * dot(f_ref[slot, k], stats[k]) + f_ref[slot, k].astype(F32)).astype(BF) for k in range(2)]
    squares = [dot(e, e) for e in es]
    f_es = [(1.25 * e.astype(F32) - square).astype(BF) for e, square in zip(es, squares)]
    ts = [(square - 2.5 * e.astype(F32)).astype(BF) for e, square in zip(es, squares)]
    f_es = [(dot(t, v) + 1.5625 * v.astype(F32)).astype(BF) for t, v in zip(ts, f_es)]
    f_es = [dot(t, v) + 1.5625 * v.astype(F32) for t, v in zip(ts, f_es)]
    ws = [(1.25 * e.astype(F32) + v).astype(BF) for e, v in zip(es, f_es)]
    xs = [1.5625 * xb_ref[slot, k].astype(F32) - dot(xb_ref[slot, k], ws[k]) for k in range(2)]
    for k in range(2):
        n_ref[0, k] = xs[k]
    left, right = (x.astype(BF) for x in xs)
    u_ref[0] = dot(dot(left, g).astype(BF), right).astype(BF)


def newton(pieces, roots, fourth):
    n_src, slots, rows, b = pieces.shape
    pair = pl.BlockSpec((1, 2, b, b), lambda i: (i, 0, 0, 0))
    return pl.pallas_call(
        newton_kernel,
        grid=(slots,),
        in_specs=[pl.BlockSpec((n_src, 1, rows, b), lambda i: (0, i, 0, 0))] + [pl.BlockSpec(memory_space=pltpu.VMEM)] * 2,
        out_specs=[pl.BlockSpec((1, b, b), lambda i: (i, 0, 0)), pair],
        out_shape=[
            jax.ShapeDtypeStruct((slots, b, b), BF),
            jax.ShapeDtypeStruct((slots, 2, b, b), F32),
        ],
        compiler_params=pltpu.CompilerParams(vmem_limit_bytes=LARGE_VMEM),
        cost_estimate=SHORT,
    )(pieces, roots, fourth)


def device(z, y, x, core):
    return ((z % 4) * 4 + y % 4) * 8 + (x % 4) * 2 + core


def chips():
    return [(z, y, x) for z in range(4) for y in range(4) for x in range(4)]


def swap_cores(v):
    return lax.ppermute(
        v, ("fsdp", "pre"), [(device(*p, c), device(*p, 1 - c)) for p in chips() for c in range(2)]
    )


def from_x(v, d):
    return lax.ppermute(
        v, ("fsdp", "pre"), [(device(z, y, x + d, c), device(z, y, x, c)) for z, y, x in chips() for c in range(2)]
    )


def from_ring(v, phase, d):
    pairs = []
    for z, y, x in chips():
        for c in range(2):
            dz, dy = (0, d) if phase == c else (d, 0)
            pairs.append((device(z + dz, y + dy, x, c), device(z, y, x, c)))
    return lax.ppermute(v, ("fsdp", "pre"), pairs)


def from_ring_across(v, d):
    pairs = []
    for z, y, x in chips():
        for c in range(2):
            dz, dy = (0, d) if c == 0 else (d, 0)
            pairs.append((device(z + dz, y + dy, x, 1 - c), device(z, y, x, c)))
    return lax.ppermute(v, ("fsdp", "pre"), pairs)


def body(inputs, grads_out, owner, offsets, prev_roots):
    slots, _, b, _ = prev_roots.shape
    tokens, cols = grads_out.shape
    half = tokens // 2
    f = lax.axis_index("fsdp").astype(jnp.int32)
    p = lax.axis_index("pre").astype(jnp.int32)
    core = p % 2
    place = jnp.stack([f // 4, f % 4, p // 2, core])
    rows_of = lambda v, c: lax.dynamic_slice_in_dim(v, c * half, half, 0)

    sent = jnp.stack([rows_of(inputs, 1 - core), rows_of(grads_out, 1 - core)])
    recv = swap_cores(sent)
    shard = jnp.stack([rows_of(grads_out, core), recv[1]])

    near = [shard, from_ring(shard, 0, 1), from_ring(shard, 0, 2), from_ring(shard, 0, 3)]
    own, other = join(near)

    mine = split_features(place, inputs, recv)
    mine = lax.all_to_all(mine, "fsdp", 0, 0, tiled=True)
    own, other, mine = lax.optimization_barrier((own, other, mine))
    mine = to_vmem(mine)
    own_1, other_3 = from_ring(own, 1, 1), from_ring(other, 1, 3)
    next_x, last_x = from_x(mine, 1), from_x(mine, 3)
    far_x = from_x(mine, 2)
    own_t, other_t, next_x, last_x = lax.optimization_barrier((own, other, next_x, last_x))
    other_1, own_3 = from_ring(other_t, 1, 1), from_ring(own_t, 1, 3)
    xb, fourth = fourth_powers(prev_roots.reshape(slots * 2, b, b))
    other_1, xb, fourth = lax.optimization_barrier((other_1, xb, fourth))
    xb, fourth = (v.reshape(prev_roots.shape) for v in (xb, fourth))
    own_2 = from_ring(own_1, 1, 1)
    far_2 = from_ring_across(other_3, 3)

    chunks = [own, other, own_1, other_1, own_3, other_3]
    share_0, share_1, acc, lhs = first_chunks(place, [mine, next_x, far_x, last_x], chunks)
    pieces = last_chunk(
        place, owner, offsets, lhs, swap_cores(lhs), own_2, far_2, acc, swap_cores(share_0), swap_cores(share_1)
    )
    pieces = lax.all_to_all(pieces, "fsdp", 0, 0, tiled=True)
    return tuple(newton(pieces.reshape(16, slots, -1, b), xb, fourth))


def solution(mesh):
    in_specs = (P("fsdp", "pre"), P("fsdp", "pre"), P(), P(), P(("fsdp", "pre"), None, None, None))
    out_specs = (P(("fsdp", "pre"), None, None), P(("fsdp", "pre"), None, None, None))
    return jax.shard_map(body, mesh=mesh, in_specs=in_specs, out_specs=out_specs, check_vma=False)
```
